32 devices in a mesh: group: 4 (over y, core), member: 8 (over z, x).
Axes of the slice: x: 2, y: 2, z: 4, core: 2. Of those that a mesh axis runs over, the one named last changes fastest.
Arguments:
- latent: bfloat16 [256, 1024], P(('group', 'member')), may hold values from -6 to 6
- out_grad: bfloat16 [256, 1024], P(('group', 'member')), may hold values from -6 to 6
- gates: bfloat16 [256, 22], P(('group', 'member')), may hold values from 0.019897461 to 0.29882812
- expert_ids: int32 [256, 22], P(('group', 'member')), may hold values from 0 to 31, all different within a row; in each aligned block of 8 rows (0 to 7, 8 to 15, ...) at most 6 rows name the same one
- up_weight: bfloat16 [8, 10752, 1024], P('member', 'group'), may hold values from -0.1875 to 0.1875
- down_weight: bfloat16 [8, 10752, 1024], P('member', 'group'), may hold values from -0.125 to 0.125
Outputs:
- latent_grad: float32 [256, 1024], P(('group', 'member'))
- up_grad: bfloat16 [8, 10752, 1024], P('member', 'group')
- down_grad: bfloat16 [8, 10752, 1024], P('member', 'group')
The draws below stay inside these ranges and needn't reach their ends.
Inputs may be any that keep to these rules, and one draw needn't show every extreme that they name: `expert_ids`: the 22 experts of a token are distinct. Among the 8 tokens of one device no expert is named more than 6 times, and in every draw some expert is named exactly 6 times by the tokens of some device.
All inputs are finite; a program needn't handle non-finite values.
Results may differ from the reference program's by a relative error of at most 0.0057.
Values may be sent and summed in bfloat16 or wider, within the bound.
No kernel may reach another device: no remote copies, remote signals or barrier semaphores. Data moves between devices by JAX's collectives and lax.ppermute only.
A program may use at most 64 MiB of HBM per device.

```python
import math
import jax
import jax.numpy as jnp
import numpy as np
from jax import lax

L = 1024
HID = 2688
TOP = 22
TOK_DEV = 8
EXP_DEV = 4
EXPERTS = 32
MOST = 6
TOKENS = 256
N_GROUP = 4
N_MEMBER = 8


def levels(key, shape, cuts, smallest, largest):
    loudness, own = 1.0, jax.random.fold_in(key, 6)
    for axis_at, shards_of in cuts:
        draws = jnp.exp(jax.random.uniform(jax.random.fold_in(own, axis_at), (shards_of,), jnp.float32, smallest / len(cuts), largest / len(cuts)))
        loudness = loudness * jnp.repeat(draws, shape[axis_at] // shards_of).reshape([-1 if axis == axis_at else 1 for axis in range(len(shape))])
    return loudness


def deal_out(stream_key, own, number, rows, amount, top, bound, lean):
    ranking = jax.random.permutation(stream_key, amount)
    heavy_load, usual = portions_of(amount, rows * top, bound, lean, True), portions_of(amount, rows * top, bound, lean, False)
    places = jnp.arange(amount)

    def named(lengths, turn):
        used = int((lengths > 0).sum())
        fixed = max(1, used // 4)
        passed = fixed + (places - fixed + turn * (used - fixed)) % max(1, amount - fixed)
        return jnp.zeros((amount,), jnp.int32).at[ranking[jnp.where(places < fixed, places, passed)]].set(jnp.asarray(lengths, jnp.int32))

    lengths = jnp.where(number % 4 == 0, named(heavy_load, number // 4), named(usual, number - number // 4 - 1))
    mixed = jax.random.permutation(jax.random.fold_in(own, 3), amount)
    giver, sink = mixed[0:amount // 2 * 2:2], mixed[1:amount // 2 * 2:2]
    slack = jnp.minimum(lengths[giver] - 1, bound - lengths[sink]) // 2
    slack = jnp.where((giver == ranking[0]) | (sink == ranking[0]) | (lengths[sink] == 0), 0, jnp.maximum(slack, 0))
    passed = jax.random.randint(jax.random.fold_in(own, 4), (amount // 2,), 0, 1 << 20) % (slack + 1)
    lengths = lengths.at[giver].add(-passed).at[sink].add(passed)
    items = jnp.searchsorted(jnp.cumsum(lengths), jnp.arange(rows * top), side="right").astype(jnp.int32)
    table = items.reshape(top, rows).T
    table = table[jax.random.permutation(jax.random.fold_in(own, 1), rows)]
    turn = jax.random.randint(jax.random.fold_in(own, 2), (rows, 1), 0, top)
    return jnp.take_along_axis(table, (jnp.arange(top)[None, :] + turn) % top, axis=1)


def portions_of(count, total, reach, lean, full):
    portions = [(1 << 20) // math.isqrt(rank ** lean) + 1 for rank in range(1, count + 1)]
    largest = reach if full else min(reach, max(-(-total // count), total * portions[0] // sum(portions)))
    least = 1 if total - largest >= count - 1 else 0
    holding, rest = [largest] + [least] * (count - 1), total - largest - least * (count - 1)
    while rest > 0:
        free = [i for i in range(1, count) if holding[i] < largest] or [i for i in range(1, count) if holding[i] < reach]
        mass, budget = sum([portions[i] for i in free]), rest
        for i in free:
            addition = min(reach - holding[i], max(1, budget * portions[i] // mass), rest)
            holding[i] = holding[i] + addition
            rest = rest - addition
    return np.array(holding)


def noise(stream_key, dims, spread, most, split=(), held_as=jnp.bfloat16):
    array = spread * jax.random.normal(stream_key, dims, jnp.float32)
    if split:
        array = array * levels(stream_key, dims, split, -0.22, 0.18)
    return jnp.clip(array, -most, most).astype(held_as)


def setup_inputs(seed: int = 0) -> dict:
    key_of = jax.random.split(jax.random.key(seed), 7)
    latent = noise(key_of[0], (TOKENS, L), 1.0, 6.0, ((0, 32),))
    out_grad = noise(key_of[1], (TOKENS, L), 1.0, 6.0, ((0, 32),))
    gates = jnp.clip(jnp.exp(math.log(0.29882812) - 2.7092764 * jax.random.uniform(key_of[2], (TOKENS, TOP), jnp.float32) ** levels(key_of[2], (TOKENS, TOP), ((0, 32),), -0.2, 0.2)), 0.019897461, 0.29882812).astype(jnp.bfloat16)
    expert_ids_keys = jax.random.split(jax.random.fold_in(key_of[3], 1), TOKENS // TOK_DEV)
    expert_ids_turns = jax.random.permutation(jax.random.fold_in(key_of[3], 3), TOKENS // TOK_DEV)
    expert_ids = jax.vmap(lambda own, number: deal_out(jax.random.fold_in(key_of[3], 2), own, number, TOK_DEV, EXPERTS, TOP, MOST, 1))(expert_ids_keys, expert_ids_turns).reshape((TOKENS, TOP))
    up_weight = noise(key_of[4], (N_MEMBER, EXP_DEV * HID, L), L ** -0.5, 0.1875, ((0, 8), (1, 4)))
    down_weight = noise(key_of[5], (N_MEMBER, EXP_DEV * HID, L), HID ** -0.5, 0.125, ((0, 8), (1, 4)))
    return {"latent": latent, "out_grad": out_grad, "gates": gates, "expert_ids": expert_ids, "up_weight": up_weight, "down_weight": down_weight}


def reference(latent, out_grad, gates, expert_ids, up_weight, down_weight):
    tokens = latent.shape[0]
    width = latent.shape[1]
    slices = N_GROUP // EXP_DEV
    slots = N_GROUP * N_MEMBER * MOST
    slice_width = HID // slices
    up_all = up_weight.reshape(EXPERTS, HID, width)
    down_all = down_weight.reshape(EXPERTS, HID, width)
    token_ids = jnp.arange(tokens, dtype=jnp.int32)
    slot_ids = jnp.arange(slots, dtype=jnp.int32)

    def one_expert(carry, inputs):
        expert, w_up, w_down = inputs
        named = expert_ids == expert
        gate = jnp.sum(jnp.where(named, gates.astype(jnp.float32), jnp.float32(0.0)), axis=1)
        chosen = jnp.any(named, axis=1).astype(jnp.int32)
        place = (jnp.cumsum(chosen) - 1).astype(jnp.int32)
        target = jnp.where(chosen > 0, place, slots).astype(jnp.int32)
        index = jnp.zeros((slots,), jnp.int32).at[target].set(token_ids, mode="drop")
        valid = (slot_ids < jnp.sum(chosen)).astype(jnp.int32)
        keep = valid[:, None] > 0
        rows_x = jnp.where(keep, latent[index].astype(jnp.float32), jnp.float32(0.0)).astype(latent.dtype)
        rows_dy = jnp.where(keep, gate[index][:, None] * out_grad[index].astype(jnp.float32), jnp.float32(0.0)).astype(latent.dtype)
        pre = jnp.dot(rows_x, w_up.T, preferred_element_type=jnp.float32)
        relu = jnp.maximum(pre, 0.0)
        act = (relu * relu).astype(latent.dtype)
        hid_grad = jnp.dot(rows_dy, w_down.T, preferred_element_type=jnp.float32)
        pre_grad = (hid_grad * 2.0 * relu).astype(latent.dtype)
        parts = jnp.einsum("rgh,ghl->grl", pre_grad.astype(jnp.float32).reshape(slots, slices, slice_width),
                           w_up.astype(jnp.float32).reshape(slices, slice_width, width),
                           precision=lax.Precision.HIGHEST)
        parts = lax.optimization_barrier(parts.astype(latent.dtype))
        row_grad = jnp.sum(parts.astype(jnp.float32), axis=0)
        row_grad = jnp.where(keep, row_grad, jnp.float32(0.0))
        carry = carry.at[index].add(row_grad)
        up_g = jnp.dot(pre_grad.T, rows_x, preferred_element_type=jnp.float32).astype(up_weight.dtype)
        down_g = jnp.dot(act.T, rows_dy, preferred_element_type=jnp.float32).astype(down_weight.dtype)
        return carry, (up_g, down_g)

    experts = jnp.arange(EXPERTS, dtype=jnp.int32)
    start = jnp.zeros((tokens, width), jnp.float32)
    latent_grad, grads = lax.scan(one_expert, start, (experts, up_all, down_all))
    up_grad = grads[0].reshape(N_MEMBER, EXP_DEV * HID, width)
    down_grad = grads[1].reshape(N_MEMBER, EXP_DEV * HID, width)
    return (latent_grad, up_grad, down_grad)
```

```python
import jax
import jax.numpy as jnp
from jax import lax
from jax.sharding import PartitionSpec as P

HID = 2688
AXES = ("group", "member")


def rounds(members, devices):
    bits = []
    bit = 1
    while bit < devices:
        if bit != members:
            bits.append(bit)
        bit *= 2
    far = members // 2
    rest = [b for b in bits if b != far]
    rest = rest[1:] + rest[:1]
    return [(far, far)] + list(zip(rest, rest[1:] + rest[:1]))


def swap(value, pair, core, devices):
    even, odd = pair
    pairs = [(i, i ^ (odd if i & core else even)) for i in range(devices)]
    return lax.ppermute(value, AXES, pairs)


def local(latent, out_grad, gates, expert_ids, up_weight, down_weight):
    width = latent.shape[1]
    slice_rows = up_weight.shape[1]
    members = lax.axis_size("member")
    groups = lax.axis_size("group")
    devices = members * groups
    local_experts = groups * slice_rows // HID
    slices = groups // local_experts
    experts = local_experts * members
    mine = lax.axis_index("member") * local_experts + lax.axis_index("group") // slices
    plan = rounds(members, devices)

    labels = jnp.arange(128, dtype=jnp.int32)
    named = expert_ids[:, :, None] == labels
    dense = jnp.sum(
        jnp.where(named, gates.astype(jnp.float32)[:, :, None], jnp.float32(0.0)), axis=1
    ).astype(jnp.bfloat16)
    packed = lax.optimization_barrier(jnp.concatenate([latent, out_grad, dense], axis=1))
    for pair in plan:
        packed = jnp.concatenate([packed, swap(packed, pair, members, devices)], axis=0)
        packed = lax.optimization_barrier(packed)
    packed = jnp.concatenate([packed, swap(packed, (members, members), members, devices)], axis=0)
    x = packed[:, :width]
    gate = jnp.sum(
        jnp.where(labels == mine, packed[:, 2 * width :].astype(jnp.float32), jnp.float32(0.0)),
        axis=1,
        keepdims=True,
    )
    dy = (gate * packed[:, width : 2 * width].astype(jnp.float32)).astype(jnp.bfloat16)

    w_up = up_weight[0]
    w_down = down_weight[0]
    pre = jnp.einsum("rl,hl->hr", x, w_up, preferred_element_type=jnp.float32)
    relu = jnp.maximum(pre, 0.0)
    act = (relu * relu).astype(jnp.bfloat16)
    hid_grad = jnp.einsum("rl,hl->hr", dy, w_down, preferred_element_type=jnp.float32)
    pre_grad = (hid_grad * 2.0 * relu).astype(jnp.bfloat16)
    part = jnp.einsum("hr,hl->rl", pre_grad, w_up, preferred_element_type=jnp.float32).astype(
        jnp.bfloat16
    )
    up_grad = jnp.einsum("hr,rl->hl", pre_grad, x, preferred_element_type=jnp.float32).astype(
        jnp.bfloat16
    )
    down_grad = jnp.einsum("hr,rl->hl", act, dy, preferred_element_type=jnp.float32).astype(
        jnp.bfloat16
    )

    half = part.shape[0] // 2
    total = part[:half].astype(jnp.float32) + swap(
        part[half:], (members, members), members, devices
    ).astype(jnp.float32)
    for pair in reversed(plan):
        half = total.shape[0] // 2
        got = swap(total[half:].astype(jnp.bfloat16), pair, members, devices)
        total = total[:half] + got.astype(jnp.float32)
    return (total, up_grad[None], down_grad[None])


def solution(mesh):
    rows = P(AXES, None)
    weights = P("member", "group", None)
    return jax.shard_map(
        local,
        mesh=mesh,
        in_specs=(rows, rows, rows, rows, weights, weights),
        out_specs=(rows, weights, weights),
        check_vma=False,
    )
```

```python
import jax
import jax.numpy as jnp
from jax import lax
from jax.experimental import pallas as pl
from jax.experimental.pallas import tpu as pltpu
from jax.sharding import PartitionSpec as P

HID = 2688
LANES = 128
AXES = ("group", "member")
BF16 = jnp.bfloat16
F32 = jnp.float32
VMEM = pl.BlockSpec(memory_space=pltpu.VMEM)
ANY = pl.BlockSpec(memory_space=pl.ANY)
HBM = pl.BlockSpec(memory_space=pltpu.HBM)
S = jax.ShapeDtypeStruct
tie = lax.optimization_barrier


def rounds(members, devices):
    bits = []
    bit = 1
    while bit < devices:
        if bit != members:
            bits.append(bit)
        bit *= 2
    far = members // 2
    rest = [b for b in bits if b != far]
    rest = rest[1:] + rest[:1]
    return [(far, far)] + list(zip(rest, rest[1:] + rest[:1]))


def swap(value, pair, core, devices):
    even, odd = pair
    pairs = [(i, i ^ (odd if i & core else even)) for i in range(devices)]
    return lax.ppermute(value, AXES, pairs)


def dot(a, b, on_a, on_b):
    return lax.dot_general(a, b, (((on_a,), (on_b,)), ((), ())), preferred_element_type=F32)


def call(kernel, out, ins, name, scratch=(), outs=None, flops=0, moved=0, limit=16, aliases={}):
    return pl.pallas_call(
        kernel,
        out_shape=out,
        in_specs=ins,
        out_specs=jax.tree.map(lambda _: VMEM, out) if outs is None else outs,
        scratch_shapes=scratch,
        name=name,
        input_output_aliases=aliases,
        compiler_params=pltpu.CompilerParams(vmem_limit_bytes=limit << 20),
        cost_estimate=pl.CostEstimate(flops=flops, bytes_accessed=moved, transcendentals=0),
    )


def pack_kernel(latent, out_grad, gates, ids, packed, latent_in, out_grad_in, gates_in, ids_in, sems):
    copies = [
        pltpu.make_async_copy(source, target, sems.at[k])
        for k, (source, target) in enumerate(
            ((ids, ids_in), (gates, gates_in), (latent, latent_in), (out_grad, out_grad_in))
        )
    ]
    for copy in copies:
        copy.start()
    copies[0].wait()
    copies[1].wait()
    rows, width = latent.shape
    lane = lax.broadcasted_iota(jnp.int32, (rows, LANES), 1)
    weight = gates_in[...].astype(F32)
    chosen = ids_in[...]
    dense = jnp.zeros(lane.shape, F32)
    for k in range(gates.shape[1]):
        dense += jnp.where(chosen[:, k : k + 1] == lane, weight[:, k : k + 1], 0.0)
    packed[:, 2 * width :] = dense.astype(BF16)
    copies[2].wait()
    packed[:, :width] = latent_in[...]
    copies[3].wait()
    packed[:, width : 2 * width] = out_grad_in[...]


def in_hbm(*arrays):
    return [pltpu.with_memory_space_constraint(array, pltpu.HBM) for array in arrays]


def pack(latent, out_grad, gates, ids):
    rows, width = latent.shape
    return call(pack_kernel, S((rows, 2 * width + LANES), BF16), [HBM] * 4, "pack",
        (pltpu.VMEM(latent.shape, BF16), pltpu.VMEM(out_grad.shape, BF16), pltpu.VMEM(gates.shape, BF16), pltpu.VMEM(ids.shape, jnp.int32),
         pltpu.SemaphoreType.DMA((4,))), limit=4)(*in_hbm(latent, out_grad, gates, ids))


def load_kernel(weight, out, sem):
    copy = pltpu.make_async_copy(weight, out, sem)
    copy.start()
    copy.wait()


def load(weight, name):
    return call(load_kernel, S(weight.shape, weight.dtype), [HBM], name, (pltpu.SemaphoreType.DMA,),
        moved=2 * weight.size, limit=8)(*in_hbm(weight))


def gated(dyg, width, rows):
    groups = lax.axis_size("group")
    local_experts = groups * rows // HID
    mine = lax.axis_index("member") * local_experts + lax.axis_index("group") // (groups // local_experts)
    gates = dyg[:, width:].astype(F32)
    lane = lax.broadcasted_iota(jnp.int32, gates.shape, 1)
    gate = jnp.sum(jnp.where(lane == mine, gates, 0.0), axis=1, keepdims=True)
    return (gate * dyg[:, :width].astype(F32)).astype(BF16)


def pre_kernel(x, w_up, relu):
    relu[...] = jnp.maximum(dot(x[...], w_up[...], 1, 1), 0.0)


def hidden_kernel(dyg, w_down, w_up, relu, row_grad, act, pre_grad, part):
    row_grad[...] = gated(dyg[...], row_grad.shape[1], w_down.shape[0])
    hid_grad = dot(row_grad[...], w_down[...], 1, 1)
    act[...] = (relu[...] * relu[...]).astype(BF16)
    pre_grad[...] = (hid_grad * 2.0 * relu[...]).astype(BF16)
    part[...] = dot(pre_grad[...], w_up[...], 1, 0).astype(BF16)


def plain(x, dyg, w_up, w_down):
    relu = jnp.maximum(dot(x, w_up, 1, 1), 0.0)
    row_grad = gated(dyg, x.shape[1], w_up.shape[0])
    act = (relu * relu).astype(BF16)
    pre_grad = (dot(row_grad, w_down, 1, 1) * 2.0 * relu).astype(BF16)
    return row_grad, act, pre_grad, dot(pre_grad, w_up, 1, 0).astype(BF16)


def outer(a, b, name, blocks, first=0, last=None, into=None):
    n, width = a.shape[1], b.shape[1]
    step = n // blocks
    last = blocks if last is None else last
    count = last - first

    def kernel(a, b, *refs):
        out, buffer, sems = refs[-3:]
        copies = []
        for k in range(count):
            at = (first + k) * step
            rows = pl.ds(k * step, step)
            buffer[rows] = dot(a[:, at : at + step], b[...], 0, 0).astype(BF16)
            copies.append(pltpu.make_async_copy(buffer.at[rows], out.at[0, pl.ds(at, step)], sems.at[k]))
            copies[-1].start()
        for copy in copies:
            copy.wait()

    args = (a, b) if into is None else (a, b, into)
    return call(kernel, S((1, n, width), BF16), [VMEM, VMEM] + [ANY] * (len(args) - 2), name,
        (pltpu.VMEM((count * step, width), BF16), pltpu.SemaphoreType.DMA((count,))), ANY,
        flops=2 * a.shape[0] * count * step * width, moved=2 * count * step * width,
        aliases={} if into is None else {2: 0})(*args)


def local(latent, out_grad, gates, expert_ids, up_weight, down_weight):
    width = latent.shape[1]
    rows = up_weight.shape[1]
    members = lax.axis_size("member")
    groups = lax.axis_size("group")
    devices = members * groups
    core = (members, members)
    plan = rounds(members, devices)
    tokens = latent.shape[0] * devices
    flops = 2 * tokens * rows * width
    small = tokens <= 256 and rows % 384 == 0
    blocks, cut = rows // 384, (4 * rows // 384 + 6) // 7
    w_up, w_down = up_weight[0], down_weight[0]

    packed = pack(latent, out_grad, gates, expert_ids)
    for k, pair in enumerate(plan[:-1]):
        if small and k == 1:
            packed, w_up = tie((packed, w_up))
        if small and k == 2:
            packed, w_down = tie((packed, w_down))
        got = swap(packed, pair, members, devices)
        if small and k == 1:
            w_up = load(w_up, "load_up")
            got, w_up = tie((got, w_up))
        if small and k == 2:
            w_down = load(w_down, "load_down")
            got, w_down = tie((got, w_down))
        packed = tie(jnp.concatenate([packed, got], axis=0))
    x, dyg = tie((packed[:, :width], packed[:, width:]))
    got_x = swap(x, plan[-1], members, devices)
    got_dyg = swap(dyg, plan[-1], members, devices)
    x = tie(jnp.concatenate([x, got_x], axis=0))
    x = jnp.concatenate([x, swap(x, core, members, devices)], axis=0)
    dyg = tie(jnp.concatenate([dyg, got_dyg], axis=0))
    x, dyg = tie((x, dyg))
    got_dyg = swap(dyg, core, members, devices)
    dyg_all = jnp.concatenate([dyg, got_dyg], axis=0)
    if small:
        relu = call(pre_kernel, S((tokens, rows), F32), [VMEM] * 2, "pre", flops=flops)(x, w_up)
        row_grad, act, pre_grad, part = call(
            hidden_kernel,
            (S((tokens, width), BF16), S((tokens, rows), BF16), S((tokens, rows), BF16), S((tokens, width), BF16)),
            [VMEM] * 4, "hidden", flops=2 * flops)(dyg_all, w_down, w_up, relu)
    else:
        row_grad, act, pre_grad, part = plain(x, dyg_all, w_up, w_down)

    half = tokens // 2
    total = part[:half].astype(F32) + swap(part[half:], core, members, devices).astype(F32)
    for k, pair in enumerate(reversed(plan)):
        half = total.shape[0] // 2
        got = swap(total[half:].astype(BF16), pair, members, devices)
        if small and k == 0:
            up_grad = outer(pre_grad, x, "up", blocks)
            got, up_grad = tie((got, up_grad))
        if small and k == 1:
            down_grad = outer(act, row_grad, "down", blocks, 0, cut)
            got, down_grad = tie((got, down_grad))
        if small and k == 2:
            down_grad = outer(act, row_grad, "down_rest", blocks, cut, blocks, down_grad)
            got, down_grad = tie((got, down_grad))
        total = total[:half] + got.astype(F32)
    if not small:
        up_grad = dot(pre_grad, x, 0, 0).astype(BF16)[None]
        down_grad = dot(act, row_grad, 0, 0).astype(BF16)[None]
    return (total, up_grad, down_grad)


def solution(mesh):
    rows = P(AXES, None)
    weights = P("member", "group", None)
    return jax.shard_map(
        local,
        mesh=mesh,
        in_specs=(rows, rows, rows, rows, weights, weights),
        out_specs=(rows, weights, weights),
        check_vma=False,
    )
```

```python
import jax
import jax.numpy as jnp
from jax import lax
from jax.experimental import pallas as pl
from jax.experimental.pallas import tpu as pltpu
from jax.sharding import PartitionSpec as P

HID = 2688
LANES = 128
AXES = ("group", "member")
BF16 = jnp.bfloat16
F32 = jnp.float32
VMEM = pl.BlockSpec(memory_space=pltpu.VMEM)
ANY = pl.BlockSpec(memory_space=pl.ANY)
HBM = pl.BlockSpec(memory_space=pltpu.HBM)
S = jax.ShapeDtypeStruct
tie = lax.optimization_barrier


def stages(members, devices):
    bits = [1 << k for k in range(1, devices.bit_length() - 1)]
    bits = [b for b in bits if b < members] + [1] + [b for b in bits if b > members]
    pairs = [bits[k : k + 2] for k in range(0, len(bits), 2)]
    return [pair if len(pair) == 1 else [pair[0], pair[1], pair[0] ^ pair[1]] for pair in pairs]


def swap(value, mask, devices):
    return lax.ppermute(value, AXES, [(i, i ^ mask) for i in range(devices)])


def dot(a, b, on_a, on_b):
    return lax.dot_general(a, b, (((on_a,), (on_b,)), ((), ())), preferred_element_type=F32)


def call(kernel, out, ins, name, scratch=(), outs=None, flops=0, moved=0, limit=16, aliases={}):
    return pl.pallas_call(
        kernel,
        out_shape=out,
        in_specs=ins,
        out_specs=jax.tree.map(lambda _: VMEM, out) if outs is None else outs,
        scratch_shapes=scratch,
        name=name,
        input_output_aliases=aliases,
        compiler_params=pltpu.CompilerParams(vmem_limit_bytes=limit << 20),
        cost_estimate=pl.CostEstimate(flops=flops, bytes_accessed=moved, transcendentals=0),
    )


def pack_kernel(latent, out_grad, gates, ids, packed, latent_in, out_grad_in, gates_in, ids_in, sems):
    copies = [
        pltpu.make_async_copy(source, target, sems.at[k])
        for k, (source, target) in enumerate(
            ((ids, ids_in), (gates, gates_in), (latent, latent_in), (out_grad, out_grad_in))
        )
    ]
    for copy in copies:
        copy.start()
    copies[0].wait()
    copies[1].wait()
    rows, width = latent.shape
    lane = lax.broadcasted_iota(jnp.int32, (rows, LANES), 1)
    weight = gates_in[...].astype(F32)
    chosen = ids_in[...]
    dense = jnp.zeros(lane.shape, F32)
    for k in range(gates.shape[1]):
        dense += jnp.where(chosen[:, k : k + 1] == lane, weight[:, k : k + 1], 0.0)
    packed[:, 2 * width :] = dense.astype(BF16)
    copies[2].wait()
    packed[:, :width] = latent_in[...]
    copies[3].wait()
    packed[:, width : 2 * width] = out_grad_in[...]


def in_hbm(*arrays):
    return [pltpu.with_memory_space_constraint(array, pltpu.HBM) for array in arrays]


def pack(latent, out_grad, gates, ids):
    rows, width = latent.shape
    return call(pack_kernel, S((rows, 2 * width + LANES), BF16), [HBM] * 4, "pack",
        (pltpu.VMEM(latent.shape, BF16), pltpu.VMEM(out_grad.shape, BF16), pltpu.VMEM(gates.shape, BF16), pltpu.VMEM(ids.shape, jnp.int32),
         pltpu.SemaphoreType.DMA((4,))), limit=4)(*in_hbm(latent, out_grad, gates, ids))


def load_kernel(weight, out, sem):
    copy = pltpu.make_async_copy(weight, out, sem)
    copy.start()
    copy.wait()


def load(weight, name):
    return call(load_kernel, S(weight.shape, weight.dtype), [HBM], name, (pltpu.SemaphoreType.DMA,),
        moved=2 * weight.size, limit=8)(*in_hbm(weight))


def gated(dyg, width, rows):
    groups = lax.axis_size("group")
    local_experts = groups * rows // HID
    mine = lax.axis_index("member") * local_experts + lax.axis_index("group") // (groups // local_experts)
    gates = dyg[:, width:].astype(F32)
    lane = lax.broadcasted_iota(jnp.int32, gates.shape, 1)
    gate = jnp.sum(jnp.where(lane == mine, gates, 0.0), axis=1, keepdims=True)
    return (gate * dyg[:, :width].astype(F32)).astype(BF16)


def pre_kernel(x, w_up, relu):
    relu[...] = jnp.maximum(dot(x[...], w_up[...], 1, 1), 0.0)


def hidden_kernel(dyg, w_down, w_up, relu, row_grad, act, pre_grad, part):
    row_grad[...] = gated(dyg[...], row_grad.shape[1], w_down.shape[0])
    hid_grad = dot(row_grad[...], w_down[...], 1, 1)
    act[...] = (relu[...] * relu[...]).astype(BF16)
    pre_grad[...] = (hid_grad * 2.0 * relu[...]).astype(BF16)
    part[...] = dot(pre_grad[...], w_up[...], 1, 0).astype(BF16)


def plain(x, dyg, w_up, w_down):
    relu = jnp.maximum(dot(x, w_up, 1, 1), 0.0)
    row_grad = gated(dyg, x.shape[1], w_up.shape[0])
    act = (relu * relu).astype(BF16)
    pre_grad = (dot(row_grad, w_down, 1, 1) * 2.0 * relu).astype(BF16)
    return row_grad, act, pre_grad, dot(pre_grad, w_up, 1, 0).astype(BF16)


def outer(a, b, name, blocks, first=0, last=None, into=None):
    n, width = a.shape[1], b.shape[1]
    step = n // blocks
    last = blocks if last is None else last
    count = last - first

    def kernel(a, b, *refs):
        out, buffer, sems = refs[-3:]
        copies = []
        for k in range(count):
            at = (first + k) * step
            rows = pl.ds(k * step, step)
            buffer[rows] = dot(a[:, at : at + step], b[...], 0, 0).astype(BF16)
            copies.append(pltpu.make_async_copy(buffer.at[rows], out.at[0, pl.ds(at, step)], sems.at[k]))
            copies[-1].start()
        for copy in copies:
            copy.wait()

    args = (a, b) if into is None else (a, b, into)
    return call(kernel, S((1, n, width), BF16), [VMEM, VMEM] + [ANY] * (len(args) - 2), name,
        (pltpu.VMEM((count * step, width), BF16), pltpu.SemaphoreType.DMA((count,))), ANY,
        flops=2 * a.shape[0] * count * step * width, moved=2 * count * step * width,
        aliases={} if into is None else {2: 0})(*args)


def local(latent, out_grad, gates, expert_ids, up_weight, down_weight):
    width = latent.shape[1]
    rows = up_weight.shape[1]
    members = lax.axis_size("member")
    groups = lax.axis_size("group")
    devices = members * groups
    core = members
    plan = stages(members, devices)
    tokens = latent.shape[0] * devices
    flops = 2 * tokens * rows * width
    small = tokens <= 256 and rows % 384 == 0
    blocks = rows // 384
    w_up, w_down = up_weight[0], down_weight[0]

    rows_all = pack(latent, out_grad, gates, expert_ids)
    for k, masks in enumerate(plan):
        if small and k == 0:
            rows_all, w_up = tie((rows_all, w_up))
        if small and k == 1:
            rows_all, w_down = tie((rows_all, w_down))
        got = [swap(rows_all, mask, devices) for mask in masks]
        if small and k == 0:
            w_up = load(w_up, "load_up")
            got[0], w_up = tie((got[0], w_up))
        if small and k == 1:
            w_down = load(w_down, "load_down")
            got[0], w_down = tie((got[0], w_down))
        rows_all = tie(jnp.concatenate([rows_all] + got, axis=0))
    x, dyg = tie((rows_all[:, :width], rows_all[:, width:]))
    x = jnp.concatenate([x, swap(x, core, devices)], axis=0)
    got_dyg = swap(dyg, core, devices)
    dyg_all = jnp.concatenate([dyg, got_dyg], axis=0)
    if small:
        relu = call(pre_kernel, S((tokens, rows), F32), [VMEM] * 2, "pre", flops=flops)(x, w_up)
        row_grad, act, pre_grad, part = call(
            hidden_kernel,
            (S((tokens, width), BF16), S((tokens, rows), BF16), S((tokens, rows), BF16), S((tokens, width), BF16)),
            [VMEM] * 4, "hidden", flops=2 * flops)(dyg_all, w_down, w_up, relu)
    else:
        row_grad, act, pre_grad, part = plain(x, dyg_all, w_up, w_down)

    half = tokens // 2
    total = part[:half].astype(F32) + swap(part[half:], core, devices).astype(F32)
    for k, masks in enumerate(reversed(plan)):
        count = total.shape[0] // (len(masks) + 1)
        cut = [total[j * count : (j + 1) * count] for j in range(len(masks) + 1)]
        got = [swap(block.astype(BF16), mask, devices) for block, mask in zip(cut[1:], masks)]
        if small and k == 0:
            up_grad = outer(pre_grad, x, "up", blocks)
            got[0], up_grad = tie((got[0], up_grad))
        if small and k == 1:
            down_grad = outer(act, row_grad, "down", blocks)
            got[0], down_grad = tie((got[0], down_grad))
        total = cut[0] + sum(block.astype(F32) for block in got)
    if not small:
        up_grad = dot(pre_grad, x, 0, 0).astype(BF16)[None]
        down_grad = dot(act, row_grad, 0, 0).astype(BF16)[None]
    return (total, up_grad, down_grad)


def solution(mesh):
    rows = P(AXES, None)
    weights = P("member", "group", None)
    return jax.shard_map(
        local,
        mesh=mesh,
        in_specs=(rows, rows, rows, rows, weights, weights),
        out_specs=(rows, weights, weights),
        check_vma=False,
    )
```

```python
import jax
import jax.numpy as jnp
from jax import lax
from jax.experimental import pallas as pl
from jax.experimental.pallas import tpu as pltpu
from jax.sharding import PartitionSpec as P

HID = 2688
LANES = 128
AXES = ("group", "member")
TIED = (0, 2, 1, 2)
BF16 = jnp.bfloat16
F32 = jnp.float32
VMEM = pl.BlockSpec(memory_space=pltpu.VMEM)
ANY = pl.BlockSpec(memory_space=pl.ANY)
HBM = pl.BlockSpec(memory_space=pltpu.HBM)
S = jax.ShapeDtypeStruct
tie = lax.optimization_barrier


def stages(members, devices):
    bits = [1 << k for k in range(1, devices.bit_length() - 1)]
    bits = [b for b in reversed(bits) if b < members] + [1] + [b for b in bits if b > members]
    pairs = [bits[k : k + 2] for k in range(0, len(bits), 2)]
    groups = [pair if len(pair) == 1 else [pair[0], pair[1], pair[0] ^ pair[1]] for pair in pairs]
    others = groups[::-1] if len(bits) % 2 == 0 else groups
    return [list(zip(even, odd)) for even, odd in zip(groups, others)]


def swap(value, masks, core, devices):
    even, odd = masks
    return lax.ppermute(value, AXES, [(i, i ^ (odd if i & core else even)) for i in range(devices)])


def dot(a, b, on_a, on_b):
    return lax.dot_general(a, b, (((on_a,), (on_b,)), ((), ())), preferred_element_type=F32)


def call(kernel, out, ins, name, scratch=(), outs=None, flops=0, moved=0, limit=16):
    return pl.pallas_call(
        kernel,
        out_shape=out,
        in_specs=ins,
        out_specs=jax.tree.map(lambda _: VMEM, out) if outs is None else outs,
        scratch_shapes=scratch,
        name=name,
        compiler_params=pltpu.CompilerParams(vmem_limit_bytes=limit << 20),
        cost_estimate=pl.CostEstimate(flops=flops, bytes_accessed=moved, transcendentals=0),
    )


def pack_kernel(latent, out_grad, gates, ids, packed, latent_in, out_grad_in, gates_in, ids_in, sems):
    copies = [
        pltpu.make_async_copy(source, target, sems.at[k])
        for k, (source, target) in enumerate(
            ((ids, ids_in), (gates, gates_in), (latent, latent_in), (out_grad, out_grad_in))
        )
    ]
    for copy in copies:
        copy.start()
    copies[0].wait()
    copies[1].wait()
    rows, width = latent.shape
    lane = lax.broadcasted_iota(jnp.int32, (rows, LANES), 1)
    weight = gates_in[...].astype(F32)
    chosen = ids_in[...]
    dense = jnp.zeros(lane.shape, F32)
    for k in range(gates.shape[1]):
        dense += jnp.where(chosen[:, k : k + 1] == lane, weight[:, k : k + 1], 0.0)
    packed[:, 2 * width :] = dense.astype(BF16)
    copies[2].wait()
    packed[:, :width] = latent_in[...]
    copies[3].wait()
    packed[:, width : 2 * width] = out_grad_in[...]


def in_hbm(*arrays):
    return [pltpu.with_memory_space_constraint(array, pltpu.HBM) for array in arrays]


def pack(latent, out_grad, gates, ids):
    rows, width = latent.shape
    return call(pack_kernel, S((rows, 2 * width + LANES), BF16), [HBM] * 4, "pack",
        (pltpu.VMEM(latent.shape, BF16), pltpu.VMEM(out_grad.shape, BF16), pltpu.VMEM(gates.shape, BF16), pltpu.VMEM(ids.shape, jnp.int32),
         pltpu.SemaphoreType.DMA((4,))), limit=4)(*in_hbm(latent, out_grad, gates, ids))


def load_kernel(weight, out, sem):
    copy = pltpu.make_async_copy(weight, out, sem)
    copy.start()
    copy.wait()


def load(weight, name):
    return call(load_kernel, S(weight.shape, weight.dtype), [HBM], name, (pltpu.SemaphoreType.DMA,),
        moved=2 * weight.size, limit=8)(*in_hbm(weight))


def gated(dyg, width, rows):
    groups = lax.axis_size("group")
    local_experts = groups * rows // HID
    mine = lax.axis_index("member") * local_experts + lax.axis_index("group") // (groups // local_experts)
    gates = dyg[:, width:].astype(F32)
    lane = lax.broadcasted_iota(jnp.int32, gates.shape, 1)
    gate = jnp.sum(jnp.where(lane == mine, gates, 0.0), axis=1, keepdims=True)
    return (gate * dyg[:, :width].astype(F32)).astype(BF16)


def pre_kernel(x, w_up, relu):
    relu[...] = jnp.maximum(dot(x[...], w_up[...], 1, 1), 0.0)


def hidden_kernel(dyg, w_down, w_up, relu, row_grad, pre_grad, part):
    row_grad[...] = gated(dyg[...], row_grad.shape[1], w_down.shape[0])
    hid_grad = dot(row_grad[...], w_down[...], 1, 1)
    pre_grad[...] = (hid_grad * 2.0 * relu[...]).astype(BF16)
    part[...] = dot(pre_grad[...], w_up[...], 1, 0).astype(BF16)


def plain(x, dyg, w_up, w_down):
    relu = jnp.maximum(dot(x, w_up, 1, 1), 0.0)
    row_grad = gated(dyg, x.shape[1], w_up.shape[0])
    act = (relu * relu).astype(BF16)
    pre_grad = (dot(row_grad, w_down, 1, 1) * 2.0 * relu).astype(BF16)
    return row_grad, act, pre_grad, dot(pre_grad, w_up, 1, 0).astype(BF16)


def outer(a, b, name, blocks):
    n, width = a.shape[1], b.shape[1]
    step = n // blocks

    def kernel(a, b, out, buffer, sems):
        copies = []
        for k in range(blocks):
            rows = pl.ds(k * step, step)
            left = a[:, k * step : (k + 1) * step]
            left = (left * left).astype(BF16) if a.dtype == F32 else left
            buffer[rows] = dot(left, b[...], 0, 0).astype(BF16)
            copies.append(pltpu.make_async_copy(buffer.at[rows], out.at[0, rows], sems.at[k]))
            copies[-1].start()
        for copy in copies:
            copy.wait()

    return call(kernel, S((1, n, width), BF16), [VMEM, VMEM], name,
        (pltpu.VMEM((n, width), BF16), pltpu.SemaphoreType.DMA((blocks,))), ANY,
        flops=2 * a.shape[0] * n * width, moved=2 * n * width)(a, b)


def local(latent, out_grad, gates, expert_ids, up_weight, down_weight):
    width = latent.shape[1]
    rows = up_weight.shape[1]
    members = lax.axis_size("member")
    groups = lax.axis_size("group")
    devices = members * groups
    core = (members, members)
    plan = stages(members, devices)
    tokens = latent.shape[0] * devices
    flops = 2 * tokens * rows * width
    small = tokens <= 256 and rows % 384 == 0
    blocks = rows // 384
    w_up, w_down = up_weight[0], down_weight[0]

    rows_all = pack(latent, out_grad, gates, expert_ids)
    for k, masks in enumerate(plan):
        if small and k == 0:
            rows_all, w_up = tie((rows_all, w_up))
        if small and k == 1:
            rows_all, w_down = tie((rows_all, w_down))
        got = [swap(rows_all, mask, members, devices) for mask in masks]
        t = TIED[k % 4]
        if small and k == 0:
            w_up = load(w_up, "load_up")
            got[t], w_up = tie((got[t], w_up))
        if small and k == 1:
            w_down = load(w_down, "load_down")
            got[t], w_down = tie((got[t], w_down))
        rows_all = tie(jnp.concatenate([rows_all] + got, axis=0))
    x, dyg = tie((rows_all[:, :width], rows_all[:, width:]))
    got_x = swap(x, core, members, devices)
    got_x, dyg = tie((got_x, dyg))
    x = jnp.concatenate([x, got_x], axis=0)
    got_dyg = swap(dyg, core, members, devices)
    dyg_all = jnp.concatenate([dyg, got_dyg], axis=0)
    if small:
        relu = call(pre_kernel, S((tokens, rows), F32), [VMEM] * 2, "pre", flops=flops)(x, w_up)
        row_grad, pre_grad, part = call(
            hidden_kernel,
            (S((tokens, width), BF16), S((tokens, rows), BF16), S((tokens, width), BF16)),
            [VMEM] * 4, "hidden", flops=2 * flops)(dyg_all, w_down, w_up, relu)
    else:
        row_grad, act, pre_grad, part = plain(x, dyg_all, w_up, w_down)

    half = tokens // 2
    total = part[:half].astype(F32) + swap(part[half:], core, members, devices).astype(F32)
    for k, masks in enumerate(reversed(plan)):
        count = total.shape[0] // (len(masks) + 1)
        cut = [total[j * count : (j + 1) * count] for j in range(len(masks) + 1)]
        got = [swap(block.astype(BF16), mask, members, devices) for block, mask in zip(cut[1:], masks)]
        t = TIED[(2 + k) % 4]
        if small and k == 0:
            up_grad = outer(pre_grad, x, "up", blocks)
            got[t], up_grad = tie((got[t], up_grad))
        if small and k == 1:
            down_grad = outer(relu, row_grad, "down", blocks)
            got[t], down_grad = tie((got[t], down_grad))
        total = cut[0] + sum(block.astype(F32) for block in got)
    if not small:
        up_grad = dot(pre_grad, x, 0, 0).astype(BF16)[None]
        down_grad = dot(act, row_grad, 0, 0).astype(BF16)[None]
    return (total, up_grad, down_grad)


def solution(mesh):
    rows = P(AXES, None)
    weights = P("member", "group", None)
    return jax.shard_map(
        local,
        mesh=mesh,
        in_specs=(rows, rows, rows, rows, weights, weights),
        out_specs=(rows, weights, weights),
        check_vma=False,
    )
```

```python
import jax
import jax.numpy as jnp
from jax import lax
from jax.experimental import pallas as pl
from jax.experimental.pallas import tpu as pltpu
from jax.sharding import PartitionSpec as P

HID = 2688
LANES = 128
AXES = ("group", "member")
TIED = (0, 2, 1, 2)
BF16 = jnp.bfloat16
F32 = jnp.float32
VMEM = pl.BlockSpec(memory_space=pltpu.VMEM)
ANY = pl.BlockSpec(memory_space=pl.ANY)
HBM = pl.BlockSpec(memory_space=pltpu.HBM)
S = jax.ShapeDtypeStruct
tie = lax.optimization_barrier


def stages(members, devices):
    bits = [1 << k for k in range(1, devices.bit_length() - 1)]
    bits = [b for b in reversed(bits) if b < members] + [1] + [b for b in bits if b > members]
    pairs = [bits[k : k + 2] for k in range(0, len(bits), 2)]
    groups = [pair if len(pair) == 1 else [pair[0], pair[1], pair[0] ^ pair[1]] for pair in pairs]
    others = groups[::-1] if len(bits) % 2 == 0 else groups
    return [list(zip(even, odd)) for even, odd in zip(groups, others)]


def swap(value, masks, core, devices):
    even, odd = masks
    return lax.ppermute(value, AXES, [(i, i ^ (odd if i & core else even)) for i in range(devices)])


def dot(a, b, on_a, on_b):
    return lax.dot_general(a, b, (((on_a,), (on_b,)), ((), ())), preferred_element_type=F32)


def call(kernel, out, ins, name, scratch=(), outs=None, flops=0, moved=0, limit=16):
    return pl.pallas_call(
        kernel,
        out_shape=out,
        in_specs=ins,
        out_specs=jax.tree.map(lambda _: VMEM, out) if outs is None else outs,
        scratch_shapes=scratch,
        name=name,
        compiler_params=pltpu.CompilerParams(vmem_limit_bytes=limit << 20),
        cost_estimate=pl.CostEstimate(flops=flops, bytes_accessed=moved, transcendentals=0),
    )


def pack_kernel(latent, out_grad, gates, ids, packed, latent_in, out_grad_in, gates_in, ids_in, sems):
    copies = [
        pltpu.make_async_copy(source, target, sems.at[k])
        for k, (source, target) in enumerate(
            ((ids, ids_in), (gates, gates_in), (latent, latent_in), (out_grad, out_grad_in))
        )
    ]
    for copy in copies:
        copy.start()
    copies[0].wait()
    copies[1].wait()
    rows, width = latent.shape
    lane = lax.broadcasted_iota(jnp.int32, (rows, LANES), 1)
    weight = gates_in[...].astype(F32)
    chosen = ids_in[...]
    dense = jnp.zeros(lane.shape, F32)
    for k in range(gates.shape[1]):
        dense += jnp.where(chosen[:, k : k + 1] == lane, weight[:, k : k + 1], 0.0)
    packed[:, 2 * width :] = dense.astype(BF16)
    copies[2].wait()
    packed[:, :width] = latent_in[...]
    copies[3].wait()
    packed[:, width : 2 * width] = out_grad_in[...]


def in_hbm(*arrays):
    return [pltpu.with_memory_space_constraint(array, pltpu.HBM) for array in arrays]


def pack(latent, out_grad, gates, ids):
    rows, width = latent.shape
    return call(pack_kernel, S((rows, 2 * width + LANES), BF16), [HBM] * 4, "pack",
        (pltpu.VMEM(latent.shape, BF16), pltpu.VMEM(out_grad.shape, BF16), pltpu.VMEM(gates.shape, BF16), pltpu.VMEM(ids.shape, jnp.int32),
         pltpu.SemaphoreType.DMA((4,))), limit=4)(*in_hbm(latent, out_grad, gates, ids))


def load(weight, name, keep):
    rows, width = weight.shape
    step = 384

    def kernel(weight, *refs):
        whole, turned, sems = refs if keep else (refs[1], refs[0], refs[2])
        copies = []
        for k in range(rows // step):
            at = pl.ds(k * step, step)
            copies.append(pltpu.make_async_copy(weight.at[at], whole.at[at], sems.at[k]))
            copies[-1].start()
        for k, copy in enumerate(copies):
            copy.wait()
            turned[:, k * step : (k + 1) * step] = whole[k * step : (k + 1) * step].T

    turned = S((width, rows), BF16)
    sems = pltpu.SemaphoreType.DMA((rows // step,))
    scratch = (sems,) if keep else (pltpu.VMEM((rows, width), BF16), sems)
    out = (S((rows, width), BF16), turned) if keep else turned
    return call(kernel, out, [HBM], name, scratch, moved=2 * weight.size)(*in_hbm(weight))


def gated(dyg, width, rows):
    groups = lax.axis_size("group")
    local_experts = groups * rows // HID
    mine = lax.axis_index("member") * local_experts + lax.axis_index("group") // (groups // local_experts)
    gates = dyg[:, width:].astype(F32)
    lane = lax.broadcasted_iota(jnp.int32, gates.shape, 1)
    gate = jnp.sum(jnp.where(lane == mine, gates, 0.0), axis=1, keepdims=True)
    return (gate * dyg[:, :width].astype(F32)).astype(BF16)


def hidden(x, dyg, up_turned, down_turned, relu, row_grad, pre_grad):
    row_grad[...] = gated(dyg[...], row_grad.shape[1], relu.shape[1])
    relu[...] = jnp.maximum(dot(x[...], up_turned[...], 1, 0), 0.0)
    hid_grad = dot(row_grad[...], down_turned[...], 1, 0)
    pre_grad[...] = (hid_grad * 2.0 * relu[...]).astype(BF16)


def hidden_part(x, dyg, up_turned, down_turned, w_up, relu, row_grad, pre_grad, part):
    hidden(x, dyg, up_turned, down_turned, relu, row_grad, pre_grad)
    part[...] = dot(pre_grad[...], w_up[...], 1, 0).astype(BF16)


def part_kernel(pre_grad, w_up, part):
    part[...] = dot(pre_grad[...], w_up[...], 1, 0)


def plain(x, dyg, w_up, w_down):
    relu = jnp.maximum(dot(x, w_up, 1, 1), 0.0)
    row_grad = gated(dyg, x.shape[1], w_up.shape[0])
    act = (relu * relu).astype(BF16)
    pre_grad = (dot(row_grad, w_down, 1, 1) * 2.0 * relu).astype(BF16)
    return row_grad, act, pre_grad, dot(pre_grad, w_up, 1, 0).astype(BF16)


def outer(a, b, name):
    n, width = a[0].shape[1], b[0].shape[1]
    step = 384
    blocks = n // step

    def kernel(a_0, a_1, b_0, b_1, out, buffer, sems):
        copies = []
        right = jnp.concatenate([b_0[...], b_1[...]], axis=0)
        for k in range(blocks):
            rows = pl.ds(k * step, step)
            left = jnp.concatenate([a_0[:, k * step : (k + 1) * step], a_1[:, k * step : (k + 1) * step]], axis=0)
            left = (left * left).astype(BF16) if left.dtype == F32 else left
            buffer[rows] = dot(left, right, 0, 0).astype(BF16)
            copies.append(pltpu.make_async_copy(buffer.at[rows], out.at[0, rows], sems.at[k]))
            copies[-1].start()
        for copy in copies:
            copy.wait()

    return call(kernel, S((1, n, width), BF16), [VMEM] * 4, name,
        (pltpu.VMEM((n, width), BF16), pltpu.SemaphoreType.DMA((blocks,))), ANY,
        flops=4 * a[0].shape[0] * n * width, moved=2 * n * width)(*a, *b)


def local(latent, out_grad, gates, expert_ids, up_weight, down_weight):
    width = latent.shape[1]
    rows = up_weight.shape[1]
    members = lax.axis_size("member")
    groups = lax.axis_size("group")
    devices = members * groups
    core = (members, members)
    plan = stages(members, devices)
    tokens = latent.shape[0] * devices
    flops = 2 * tokens * rows * width
    small = tokens <= 256 and rows % 384 == 0
    w_up, w_down = up_weight[0], down_weight[0]

    rows_all = pack(latent, out_grad, gates, expert_ids)
    for k, masks in enumerate(plan):
        if small and k == 0:
            rows_all, w_up = tie((rows_all, w_up))
        if small and k == 1:
            rows_all, w_down = tie((rows_all, w_down))
        got = [swap(rows_all, mask, members, devices) for mask in masks]
        t = TIED[k % 4]
        if small and k == 0:
            w_up, up_turned = load(w_up, "load_up", True)
            got[t], w_up, up_turned = tie((got[t], w_up, up_turned))
        if small and k == 1:
            down_turned = load(w_down, "load_down", False)
            got[t], down_turned = tie((got[t], down_turned))
        rows_all = tie(jnp.concatenate([rows_all] + got, axis=0))
    x, dyg = tie((rows_all[:, :width], rows_all[:, width:]))
    got_x = swap(x, core, members, devices)
    got_dyg = swap(dyg, core, members, devices)
    half = tokens // 2
    if small:
        outs = (S((half, rows), F32), S((half, width), BF16), S((half, rows), BF16))
        left = call(hidden, outs, [VMEM] * 4, "hidden", flops=flops)(x, dyg, up_turned, down_turned)
        got_x, left = tie((got_x, left))
        right = call(hidden_part, (*outs, S((half, width), BF16)), [VMEM] * 5, "hidden_part", flops=3 * flops // 2)(
            got_x, got_dyg, up_turned, down_turned, w_up)
        got = swap(right[3], core, members, devices)
        ours = call(part_kernel, S((half, width), F32), [VMEM] * 2, "part", flops=flops // 2)(left[2], w_up)
        x, relu, row_grad, pre_grad = (x, got_x), (left[0], right[0]), (left[1], right[1]), (left[2], right[2])
    else:
        x, dyg = jnp.concatenate([x, got_x]), jnp.concatenate([dyg, got_dyg])
        row_grad, act, pre_grad, part = plain(x, dyg, w_up, w_down)
        ours = part[:half].astype(F32)
        got = swap(part[half:], core, members, devices)

    total = ours + got.astype(F32)
    for k, masks in enumerate(reversed(plan)):
        count = total.shape[0] // (len(masks) + 1)
        cut = [total[j * count : (j + 1) * count] for j in range(len(masks) + 1)]
        got = [swap(block.astype(BF16), mask, members, devices) for block, mask in zip(cut[1:], masks)]
        t = TIED[(2 + k) % 4]
        if small and k == 0:
            up_grad = outer(pre_grad, x, "up")
            got[t], up_grad = tie((got[t], up_grad))
        if small and k == 1:
            down_grad = outer(relu, row_grad, "down")
            got[t], down_grad = tie((got[t], down_grad))
        total = cut[0] + sum(block.astype(F32) for block in got)
    if not small:
        up_grad = dot(pre_grad, x, 0, 0).astype(BF16)[None]
        down_grad = dot(act, row_grad, 0, 0).astype(BF16)[None]
    return (total, up_grad, down_grad)


def solution(mesh):
    rows = P(AXES, None)
    weights = P("member", "group", None)
    return jax.shard_map(
        local,
        mesh=mesh,
        in_specs=(rows, rows, rows, rows, weights, weights),
        out_specs=(rows, weights, weights),
        check_vma=False,
    )
```

```python
import jax
import jax.numpy as jnp
from jax import lax
from jax.experimental import pallas as pl
from jax.experimental.pallas import tpu as pltpu
from jax.sharding import PartitionSpec as P

HID = 2688
LANES = 128
AXES = ("group", "member")
TIED = (0, 2, 1, 2)
BF16 = jnp.bfloat16
F32 = jnp.float32
VMEM = pl.BlockSpec(memory_space=pltpu.VMEM)
ANY = pl.BlockSpec(memory_space=pl.ANY)
HBM = pl.BlockSpec(memory_space=pltpu.HBM)
S = jax.ShapeDtypeStruct
tie = lax.optimization_barrier


def stages(members, devices):
    bits = [1 << k for k in range(1, devices.bit_length() - 1)]
    bits = [b for b in reversed(bits) if b < members] + [1] + [b for b in bits if b > members]
    pairs = [bits[k : k + 2] for k in range(0, len(bits), 2)]
    groups = [pair if len(pair) == 1 else [pair[0], pair[1], pair[0] ^ pair[1]] for pair in pairs]
    others = groups[::-1] if len(bits) % 2 == 0 else groups
    return [list(zip(even, odd)) for even, odd in zip(groups, others)]


def swap(value, masks, core, devices):
    even, odd = masks
    return lax.ppermute(value, AXES, [(i, i ^ (odd if i & core else even)) for i in range(devices)])


def dot(a, b, on_a, on_b):
    return lax.dot_general(a, b, (((on_a,), (on_b,)), ((), ())), preferred_element_type=F32)


def call(kernel, out, ins, name, scratch=(), outs=None, flops=0, moved=0, limit=16):
    return pl.pallas_call(
        kernel,
        out_shape=out,
        in_specs=ins,
        out_specs=jax.tree.map(lambda _: VMEM, out) if outs is None else outs,
        scratch_shapes=scratch,
        name=name,
        compiler_params=pltpu.CompilerParams(vmem_limit_bytes=limit << 20),
        cost_estimate=pl.CostEstimate(flops=flops, bytes_accessed=moved, transcendentals=0),
    )


def pack_kernel(latent, out_grad, gates, ids, packed, latent_in, out_grad_in, gates_in, ids_in, sems):
    copies = [
        pltpu.make_async_copy(source, target, sems.at[k])
        for k, (source, target) in enumerate(
            ((ids, ids_in), (gates, gates_in), (latent, latent_in), (out_grad, out_grad_in))
        )
    ]
    for copy in copies:
        copy.start()
    copies[0].wait()
    copies[1].wait()
    rows, width = latent.shape
    lane = lax.broadcasted_iota(jnp.int32, (rows, LANES), 1)
    weight = gates_in[...].astype(F32)
    chosen = ids_in[...]
    dense = jnp.zeros(lane.shape, F32)
    for k in range(gates.shape[1]):
        dense += jnp.where(chosen[:, k : k + 1] == lane, weight[:, k : k + 1], 0.0)
    packed[:, 2 * width :] = dense.astype(BF16)
    copies[2].wait()
    packed[:, :width] = latent_in[...]
    copies[3].wait()
    packed[:, width : 2 * width] = out_grad_in[...]


def in_hbm(*arrays):
    return [pltpu.with_memory_space_constraint(array, pltpu.HBM) for array in arrays]


def pack(latent, out_grad, gates, ids):
    rows, width = latent.shape
    return call(pack_kernel, S((rows, 2 * width + LANES), BF16), [HBM] * 4, "pack",
        (pltpu.VMEM(latent.shape, BF16), pltpu.VMEM(out_grad.shape, BF16), pltpu.VMEM(gates.shape, BF16), pltpu.VMEM(ids.shape, jnp.int32),
         pltpu.SemaphoreType.DMA((4,))), limit=4)(*in_hbm(latent, out_grad, gates, ids))


def load(weight, name, keep):
    rows, width = weight.shape
    step = 384

    def kernel(weight, *refs):
        whole, turned, sems = refs if keep else (refs[1], refs[0], refs[2])
        copies = []
        for k in range(rows // step):
            at = pl.ds(k * step, step)
            copies.append(pltpu.make_async_copy(weight.at[at], whole.at[at], sems.at[k]))
            copies[-1].start()
        for k, copy in enumerate(copies):
            copy.wait()
            turned[:, k * step : (k + 1) * step] = whole[k * step : (k + 1) * step].T

    turned = S((width, rows), BF16)
    sems = pltpu.SemaphoreType.DMA((rows // step,))
    scratch = (sems,) if keep else (pltpu.VMEM((rows, width), BF16), sems)
    out = (S((rows, width), BF16), turned) if keep else turned
    return call(kernel, out, [HBM], name, scratch, moved=2 * weight.size)(*in_hbm(weight))


def gated(dyg, width, rows):
    groups = lax.axis_size("group")
    local_experts = groups * rows // HID
    mine = lax.axis_index("member") * local_experts + lax.axis_index("group") // (groups // local_experts)
    gates = dyg[:, width:].astype(F32)
    lane = lax.broadcasted_iota(jnp.int32, gates.shape, 1)
    gate = jnp.sum(jnp.where(lane == mine, gates, 0.0), axis=1, keepdims=True)
    return (gate * dyg[:, :width].astype(F32)).astype(BF16)


def hidden(rows, up_turned, down_turned, relu, row_grad, pre_grad):
    width = row_grad.shape[1]
    row_grad[...] = gated(rows[:, width:], width, relu.shape[1])
    relu[...] = jnp.maximum(dot(rows[:, :width], up_turned[...], 1, 0), 0.0)
    hid_grad = dot(row_grad[...], down_turned[...], 1, 0)
    pre_grad[...] = (hid_grad * 2.0 * relu[...]).astype(BF16)


def hidden_part(rows, up_turned, down_turned, w_up, relu, row_grad, pre_grad, part):
    hidden(rows, up_turned, down_turned, relu, row_grad, pre_grad)
    part[...] = dot(pre_grad[...], w_up[...], 1, 0).astype(BF16)


def part_kernel(pre_grad, w_up, part):
    part[...] = dot(pre_grad[...], w_up[...], 1, 0)


def plain(x, dyg, w_up, w_down):
    relu = jnp.maximum(dot(x, w_up, 1, 1), 0.0)
    row_grad = gated(dyg, x.shape[1], w_up.shape[0])
    act = (relu * relu).astype(BF16)
    pre_grad = (dot(row_grad, w_down, 1, 1) * 2.0 * relu).astype(BF16)
    return row_grad, act, pre_grad, dot(pre_grad, w_up, 1, 0).astype(BF16)


def outer(lefts, rights, width, name):
    n = lefts[0].shape[1]
    step = 384
    blocks = n // step

    def kernel(*refs):
        left_refs, right_refs = refs[: len(lefts)], refs[len(lefts) : len(lefts) + len(rights)]
        out, buffer, sems = refs[-3:]
        copies = []
        right = jnp.concatenate([ref[:, :width] for ref in right_refs], axis=0)
        for k in range(blocks):
            rows = pl.ds(k * step, step)
            left = jnp.concatenate([ref[:, k * step : (k + 1) * step] for ref in left_refs], axis=0)
            left = (left * left).astype(BF16) if left.dtype == F32 else left
            buffer[rows] = dot(left, right, 0, 0).astype(BF16)
            copies.append(pltpu.make_async_copy(buffer.at[rows], out.at[0, rows], sems.at[k]))
            copies[-1].start()
        for copy in copies:
            copy.wait()

    return call(kernel, S((1, n, width), BF16), [VMEM] * (len(lefts) + len(rights)), name,
        (pltpu.VMEM((n, width), BF16), pltpu.SemaphoreType.DMA((blocks,))), ANY,
        flops=2 * sum(left.shape[0] for left in lefts) * n * width, moved=2 * n * width)(*lefts, *rights)


def local(latent, out_grad, gates, expert_ids, up_weight, down_weight):
    width = latent.shape[1]
    rows = up_weight.shape[1]
    members = lax.axis_size("member")
    groups = lax.axis_size("group")
    devices = members * groups
    core = (members, members)
    plan = stages(members, devices)
    tokens = latent.shape[0] * devices
    flops = 2 * tokens * rows * width
    small = tokens == 256 and rows % 384 == 0 and len(plan) == 2
    w_up, w_down = up_weight[0], down_weight[0]

    half = tokens // 2
    rows_all = pack(latent, out_grad, gates, expert_ids)
    if not small:
        for masks in plan:
            got = [swap(rows_all, mask, members, devices) for mask in masks]
            rows_all = jnp.concatenate([rows_all] + got, axis=0)
        rows_all = jnp.concatenate([rows_all, swap(rows_all, core, members, devices)], axis=0)
        x = rows_all[:, :width]
        row_grad, act, pre_grad, part = plain(x, rows_all[:, width:], w_up, w_down)
        ours = part[:half].astype(F32)
        got = swap(part[half:], core, members, devices)
    else:
        outs = (S((half, rows), F32), S((half, width), BF16), S((half, rows), BF16))
        rows_all, w_up = tie((rows_all, w_up))
        got = [swap(rows_all, mask, members, devices) for mask in plan[0]]
        w_up, up_turned = load(w_up, "load_up", True)
        got[TIED[0]], w_up, up_turned = tie((got[TIED[0]], w_up, up_turned))
        rows_all = tie(jnp.concatenate([rows_all] + got, axis=0))

        rows_all, w_down = tie((rows_all, w_down))
        got = [swap(rows_all, mask, members, devices) for mask in plan[1]]
        down_turned = load(w_down, "load_down", False)
        got[TIED[1]], down_turned = tie((got[TIED[1]], down_turned))
        rows_all = tie(jnp.concatenate([rows_all] + got, axis=0))

        theirs = swap(rows_all, core, members, devices)
        first = call(hidden, outs, [VMEM] * 3, "hidden", flops=flops)(rows_all, up_turned, down_turned)
        theirs, first = tie((theirs, first))
        second = call(hidden_part, (*outs, S((half, width), BF16)), [VMEM] * 4, "hidden_part", flops=3 * flops // 2)(
            theirs, up_turned, down_turned, w_up)
        got = swap(second[3], core, members, devices)
        ours = call(part_kernel, S((half, width), F32), [VMEM] * 2, "part", flops=flops // 2)(first[2], w_up)
        x = (rows_all, theirs)
        relu, row_grad, pre_grad = ((first[k], second[k]) for k in range(3))

    total = ours + got.astype(F32)
    for k, masks in enumerate(reversed(plan)):
        count = total.shape[0] // (len(masks) + 1)
        cut = [total[j * count : (j + 1) * count] for j in range(len(masks) + 1)]
        got = [swap(block.astype(BF16), mask, members, devices) for block, mask in zip(cut[1:], masks)]
        t = TIED[(2 + k) % 4]
        if small and k == 0:
            up_grad = outer(pre_grad, x, width, "up")
            got[t], up_grad = tie((got[t], up_grad))
        if small and k == 1:
            down_grad = outer(relu, row_grad, width, "down")
            got[t], down_grad = tie((got[t], down_grad))
        total = cut[0] + sum(block.astype(F32) for block in got)
    if not small:
        up_grad = dot(pre_grad, x, 0, 0).astype(BF16)[None]
        down_grad = dot(act, row_grad, 0, 0).astype(BF16)[None]
    return (total, up_grad, down_grad)


def solution(mesh):
    rows = P(AXES, None)
    weights = P("member", "group", None)
    return jax.shard_map(
        local,
        mesh=mesh,
        in_specs=(rows, rows, rows, rows, weights, weights),
        out_specs=(rows, weights, weights),
        check_vma=False,
    )
```

```python
import jax
import jax.numpy as jnp
from jax import lax
from jax.experimental import pallas as pl
from jax.experimental.pallas import tpu as pltpu
from jax.sharding import PartitionSpec as P

HID = 2688
LANES = 128
AXES = ("group", "member")
TIED = (0, 2, 1, 2)
BF16 = jnp.bfloat16
F32 = jnp.float32
VMEM = pl.BlockSpec(memory_space=pltpu.VMEM)
ANY = pl.BlockSpec(memory_space=pl.ANY)
HBM = pl.BlockSpec(memory_space=pltpu.HBM)
S = jax.ShapeDtypeStruct
tie = lax.optimization_barrier


def stages(members, devices):
    bits = [1 << k for k in range(1, devices.bit_length() - 1)]
    bits = [b for b in reversed(bits) if b < members] + [1] + [b for b in bits if b > members]
    pairs = [bits[k : k + 2] for k in range(0, len(bits), 2)]
    groups = [pair if len(pair) == 1 else [pair[0], pair[1], pair[0] ^ pair[1]] for pair in pairs]
    others = groups[::-1] if len(bits) % 2 == 0 else groups
    return [list(zip(even, odd)) for even, odd in zip(groups, others)]


def swap(value, masks, core, devices):
    even, odd = masks
    return lax.ppermute(value, AXES, [(i, i ^ (odd if i & core else even)) for i in range(devices)])


def dot(a, b, on_a, on_b):
    return lax.dot_general(a, b, (((on_a,), (on_b,)), ((), ())), preferred_element_type=F32)


def call(kernel, out, ins, name, scratch=(), outs=None, flops=0, moved=0, limit=16):
    return pl.pallas_call(
        kernel,
        out_shape=out,
        in_specs=ins,
        out_specs=jax.tree.map(lambda _: VMEM, out) if outs is None else outs,
        scratch_shapes=scratch,
        name=name,
        compiler_params=pltpu.CompilerParams(vmem_limit_bytes=limit << 20),
        cost_estimate=pl.CostEstimate(flops=flops, bytes_accessed=moved, transcendentals=0),
    )


def pack_kernel(latent, out_grad, gates, ids, packed, latent_in, out_grad_in, gates_in, ids_in, lists, sems):
    copies = [
        pltpu.make_async_copy(source, target, sems.at[k])
        for k, (source, target) in enumerate(
            ((ids, ids_in), (gates, gates_in), (latent, latent_in), (out_grad, out_grad_in))
        )
    ]
    for copy in copies:
        copy.start()
    copies[0].wait()
    copies[1].wait()
    rows, width = latent.shape
    top = gates.shape[1]
    lists[...] = jnp.zeros_like(lists)
    lists[:, :top] = gates_in[...].astype(F32)
    lists[:, LANES // 2 : LANES // 2 + top] = (ids_in[...] + 1).astype(F32)
    packed[:, 2 * width :] = lists[...].astype(BF16)
    copies[2].wait()
    packed[:, :width] = latent_in[...]
    copies[3].wait()
    packed[:, width : 2 * width] = out_grad_in[...]


def in_hbm(*arrays):
    return [pltpu.with_memory_space_constraint(array, pltpu.HBM) for array in arrays]


def pack(latent, out_grad, gates, ids):
    rows, width = latent.shape
    return call(pack_kernel, S((rows, 2 * width + LANES), BF16), [HBM] * 4, "pack",
        (pltpu.VMEM(latent.shape, BF16), pltpu.VMEM(out_grad.shape, BF16), pltpu.VMEM(gates.shape, BF16), pltpu.VMEM(ids.shape, jnp.int32),
         pltpu.VMEM((rows, LANES), F32), pltpu.SemaphoreType.DMA((4,))), limit=4)(*in_hbm(latent, out_grad, gates, ids))


def load(weight, name, keep):
    rows, width = weight.shape
    step = 384

    def kernel(weight, *refs):
        whole, turned, sems = refs if keep else (refs[1], refs[0], refs[2])
        copies = []
        for k in range(rows // step):
            at = pl.ds(k * step, step)
            copies.append(pltpu.make_async_copy(weight.at[at], whole.at[at], sems.at[k]))
            copies[-1].start()
        for k, copy in enumerate(copies):
            copy.wait()
            turned[:, k * step : (k + 1) * step] = whole[k * step : (k + 1) * step].T

    turned = S((width, rows), BF16)
    sems = pltpu.SemaphoreType.DMA((rows // step,))
    scratch = (sems,) if keep else (pltpu.VMEM((rows, width), BF16), sems)
    out = (S((rows, width), BF16), turned) if keep else turned
    return call(kernel, out, [HBM], name, scratch, moved=2 * weight.size)(*in_hbm(weight))


def gated(dyg, width, rows):
    groups = lax.axis_size("group")
    local_experts = groups * rows // HID
    mine = lax.axis_index("member") * local_experts + lax.axis_index("group") // (groups // local_experts)
    lists = dyg[:, width:].astype(F32)
    named = lists[:, LANES // 2 :] == (mine + 1).astype(F32)
    gate = jnp.sum(jnp.where(named, lists[:, : LANES // 2], 0.0), axis=1, keepdims=True)
    return (gate * dyg[:, :width].astype(F32)).astype(BF16)


def hidden(rows, up_turned, down_turned, relu, row_grad, pre_grad):
    width = row_grad.shape[1]
    row_grad[...] = gated(rows[:, width:], width, relu.shape[1])
    relu[...] = jnp.maximum(dot(rows[:, :width], up_turned[...], 1, 0), 0.0)
    hid_grad = dot(row_grad[...], down_turned[...], 1, 0)
    pre_grad[...] = (hid_grad * 2.0 * relu[...]).astype(BF16)


def hidden_part(rows, up_turned, down_turned, w_up, relu, row_grad, pre_grad, part):
    hidden(rows, up_turned, down_turned, relu, row_grad, pre_grad)
    part[...] = dot(pre_grad[...], w_up[...], 1, 0).astype(BF16)


def part_kernel(pre_grad, w_up, part):
    part[...] = dot(pre_grad[...], w_up[...], 1, 0)


def plain(x, dyg, w_up, w_down):
    relu = jnp.maximum(dot(x, w_up, 1, 1), 0.0)
    row_grad = gated(dyg, x.shape[1], w_up.shape[0])
    act = (relu * relu).astype(BF16)
    pre_grad = (dot(row_grad, w_down, 1, 1) * 2.0 * relu).astype(BF16)
    return row_grad, act, pre_grad, dot(pre_grad, w_up, 1, 0).astype(BF16)


def outer(lefts, rights, width, name):
    n = lefts[0].shape[1]
    step = 384
    blocks = n // step

    def kernel(*refs):
        left_refs, right_refs = refs[: len(lefts)], refs[len(lefts) : len(lefts) + len(rights)]
        out, buffer, sems = refs[-3:]
        copies = []
        right = jnp.concatenate([ref[:, :width] for ref in right_refs], axis=0)
        for k in range(blocks):
            rows = pl.ds(k * step, step)
            left = jnp.concatenate([ref[:, k * step : (k + 1) * step] for ref in left_refs], axis=0)
            left = (left * left).astype(BF16) if left.dtype == F32 else left
            buffer[rows] = dot(left, right, 0, 0).astype(BF16)
            copies.append(pltpu.make_async_copy(buffer.at[rows], out.at[0, rows], sems.at[k]))
            copies[-1].start()
        for copy in copies:
            copy.wait()

    return call(kernel, S((1, n, width), BF16), [VMEM] * (len(lefts) + len(rights)), name,
        (pltpu.VMEM((n, width), BF16), pltpu.SemaphoreType.DMA((blocks,))), ANY,
        flops=2 * sum(left.shape[0] for left in lefts) * n * width, moved=2 * n * width)(*lefts, *rights)


def local(latent, out_grad, gates, expert_ids, up_weight, down_weight):
    width = latent.shape[1]
    rows = up_weight.shape[1]
    members = lax.axis_size("member")
    groups = lax.axis_size("group")
    devices = members * groups
    core = (members, members)
    plan = stages(members, devices)
    tokens = latent.shape[0] * devices
    flops = 2 * tokens * rows * width
    small = tokens == 256 and rows % 384 == 0 and len(plan) == 2
    w_up, w_down = up_weight[0], down_weight[0]

    half = tokens // 2
    rows_all = pack(latent, out_grad, gates, expert_ids)
    if not small:
        for masks in plan:
            got = [swap(rows_all, mask, members, devices) for mask in masks]
            rows_all = jnp.concatenate([rows_all] + got, axis=0)
        rows_all = jnp.concatenate([rows_all, swap(rows_all, core, members, devices)], axis=0)
        x = rows_all[:, :width]
        row_grad, act, pre_grad, part = plain(x, rows_all[:, width:], w_up, w_down)
        ours = part[:half].astype(F32)
        got = swap(part[half:], core, members, devices)
    else:
        outs = (S((half, rows), F32), S((half, width), BF16), S((half, rows), BF16))
        rows_all, w_up = tie((rows_all, w_up))
        got = [swap(rows_all, mask, members, devices) for mask in plan[0]]
        w_up, up_turned = load(w_up, "load_up", True)
        got[TIED[0]], w_up, up_turned = tie((got[TIED[0]], w_up, up_turned))
        rows_all = tie(jnp.concatenate([rows_all] + got, axis=0))

        rows_all, w_down = tie((rows_all, w_down))
        got = [swap(rows_all, mask, members, devices) for mask in plan[1]]
        down_turned = load(w_down, "load_down", False)
        got[TIED[1]], down_turned = tie((got[TIED[1]], down_turned))
        rows_all = tie(jnp.concatenate([rows_all] + got, axis=0))

        theirs = swap(rows_all, core, members, devices)
        first = call(hidden, outs, [VMEM] * 3, "hidden", flops=flops)(rows_all, up_turned, down_turned)
        theirs, first = tie((theirs, first))
        second = call(hidden_part, (*outs, S((half, width), BF16)), [VMEM] * 4, "hidden_part", flops=3 * flops // 2)(
            theirs, up_turned, down_turned, w_up)
        got = swap(second[3], core, members, devices)
        ours = call(part_kernel, S((half, width), F32), [VMEM] * 2, "part", flops=flops // 2)(first[2], w_up)
        x = (rows_all, theirs)
        relu, row_grad, pre_grad = ((first[k], second[k]) for k in range(3))

    total = ours + got.astype(F32)
    for k, masks in enumerate(reversed(plan)):
        count = total.shape[0] // (len(masks) + 1)
        cut = [total[j * count : (j + 1) * count] for j in range(len(masks) + 1)]
        got = [swap(block.astype(BF16), mask, members, devices) for block, mask in zip(cut[1:], masks)]
        t = TIED[(2 + k) % 4]
        if small and k == 0:
            up_grad = outer(pre_grad, x, width, "up")
            got[t], up_grad = tie((got[t], up_grad))
        if small and k == 1:
            down_grad = outer(relu, row_grad, width, "down")
            got[t], down_grad = tie((got[t], down_grad))
        total = cut[0] + sum(block.astype(F32) for block in got)
    if not small:
        up_grad = dot(pre_grad, x, 0, 0).astype(BF16)[None]
        down_grad = dot(act, row_grad, 0, 0).astype(BF16)[None]
    return (total, up_grad, down_grad)


def solution(mesh):
    rows = P(AXES, None)
    weights = P("member", "group", None)
    return jax.shard_map(
        local,
        mesh=mesh,
        in_specs=(rows, rows, rows, rows, weights, weights),
        out_specs=(rows, weights, weights),
        check_vma=False,
    )
```

```python
import jax
import jax.numpy as jnp
from jax import lax
from jax.experimental import pallas as pl
from jax.experimental.pallas import tpu as pltpu
from jax.sharding import PartitionSpec as P

HID = 2688
LANES = 128
AXES = ("group", "member")
TIED = (0, 2, 1, 1)
BF16 = jnp.bfloat16
F32 = jnp.float32
VMEM = pl.BlockSpec(memory_space=pltpu.VMEM)
ANY = pl.BlockSpec(memory_space=pl.ANY)
HBM = pl.BlockSpec(memory_space=pltpu.HBM)
S = jax.ShapeDtypeStruct
tie = lax.optimization_barrier


def stages(members, devices):
    bits = [1 << k for k in range(1, devices.bit_length() - 1)]
    bits = [b for b in reversed(bits) if b < members] + [1] + [b for b in bits if b > members]
    pairs = [bits[k : k + 2] for k in range(0, len(bits), 2)]
    groups = [pair if len(pair) == 1 else [pair[0], pair[1], pair[0] ^ pair[1]] for pair in pairs]
    others = groups[::-1] if len(bits) % 2 == 0 else groups
    return [list(zip(even, odd)) for even, odd in zip(groups, others)]


def swap(value, masks, core, devices):
    even, odd = masks
    return lax.ppermute(value, AXES, [(i, i ^ (odd if i & core else even)) for i in range(devices)])


def dot(a, b, on_a, on_b):
    return lax.dot_general(a, b, (((on_a,), (on_b,)), ((), ())), preferred_element_type=F32)


def call(kernel, out, ins, name, scratch=(), outs=None, flops=0, moved=0, limit=16):
    return pl.pallas_call(
        kernel,
        out_shape=out,
        in_specs=ins,
        out_specs=jax.tree.map(lambda _: VMEM, out) if outs is None else outs,
        scratch_shapes=scratch,
        name=name,
        compiler_params=pltpu.CompilerParams(vmem_limit_bytes=limit << 20),
        cost_estimate=pl.CostEstimate(flops=flops, bytes_accessed=moved, transcendentals=0),
    )


def pack_kernel(latent, out_grad, gates, ids, packed, latent_in, out_grad_in, gates_in, ids_in, sems):
    copies = [
        pltpu.make_async_copy(source, target, sems.at[k])
        for k, (source, target) in enumerate(
            ((ids, ids_in), (gates, gates_in), (latent, latent_in), (out_grad, out_grad_in))
        )
    ]
    for copy in copies:
        copy.start()
    copies[0].wait()
    copies[1].wait()
    rows, width = latent.shape
    lane = lax.broadcasted_iota(jnp.int32, (rows, LANES), 1)
    weight = gates_in[...].astype(F32)
    chosen = ids_in[...]
    dense = jnp.zeros(lane.shape, F32)
    for k in range(gates.shape[1]):
        dense += jnp.where(chosen[:, k : k + 1] == lane, weight[:, k : k + 1], 0.0)
    packed[:, 2 * width :] = dense.astype(BF16)
    copies[2].wait()
    packed[:, :width] = latent_in[...]
    copies[3].wait()
    packed[:, width : 2 * width] = out_grad_in[...]


def in_hbm(*arrays):
    return [pltpu.with_memory_space_constraint(array, pltpu.HBM) for array in arrays]


def pack(latent, out_grad, gates, ids):
    rows, width = latent.shape
    return call(pack_kernel, S((rows, 2 * width + LANES), BF16), [HBM] * 4, "pack",
        (pltpu.VMEM(latent.shape, BF16), pltpu.VMEM(out_grad.shape, BF16), pltpu.VMEM(gates.shape, BF16), pltpu.VMEM(ids.shape, jnp.int32),
         pltpu.SemaphoreType.DMA((4,))), limit=4)(*in_hbm(latent, out_grad, gates, ids))


def load(weight, name, keep):
    rows, width = weight.shape
    step = 384

    def kernel(weight, *refs):
        whole, turned, sems = refs if keep else (refs[1], refs[0], refs[2])
        copies = []
        for k in range(rows // step):
            at = pl.ds(k * step, step)
            copies.append(pltpu.make_async_copy(weight.at[at], whole.at[at], sems.at[k]))
            copies[-1].start()
        for k, copy in enumerate(copies):
            copy.wait()
            turned[:, k * step : (k + 1) * step] = whole[k * step : (k + 1) * step].T

    turned = S((width, rows), BF16)
    sems = pltpu.SemaphoreType.DMA((rows // step,))
    scratch = (sems,) if keep else (pltpu.VMEM((rows, width), BF16), sems)
    out = (S((rows, width), BF16), turned) if keep else turned
    return call(kernel, out, [HBM], name, scratch, moved=2 * weight.size)(*in_hbm(weight))


def gated(dyg, width, rows):
    groups = lax.axis_size("group")
    local_experts = groups * rows // HID
    mine = lax.axis_index("member") * local_experts + lax.axis_index("group") // (groups // local_experts)
    gates = dyg[:, width:].astype(F32)
    lane = lax.broadcasted_iota(jnp.int32, gates.shape, 1)
    gate = jnp.sum(jnp.where(lane == mine, gates, 0.0), axis=1, keepdims=True)
    return (gate * dyg[:, :width].astype(F32)).astype(BF16)


def hidden(rows, up_turned, down_turned, relu, row_grad, pre_grad):
    width = row_grad.shape[1]
    row_grad[...] = gated(rows[:, width:], width, relu.shape[1])
    relu[...] = jnp.maximum(dot(rows[:, :width], up_turned[...], 1, 0), 0.0)
    hid_grad = dot(row_grad[...], down_turned[...], 1, 0)
    pre_grad[...] = (hid_grad * 2.0 * relu[...]).astype(BF16)


def hidden_part(rows, up_turned, down_turned, w_up, relu, row_grad, pre_grad, part):
    hidden(rows, up_turned, down_turned, relu, row_grad, pre_grad)
    part[...] = dot(pre_grad[...], w_up[...], 1, 0).astype(BF16)


def part_kernel(pre_grad, w_up, part):
    part[...] = dot(pre_grad[...], w_up[...], 1, 0)


def plain(x, dyg, w_up, w_down):
    relu = jnp.maximum(dot(x, w_up, 1, 1), 0.0)
    row_grad = gated(dyg, x.shape[1], w_up.shape[0])
    act = (relu * relu).astype(BF16)
    pre_grad = (dot(row_grad, w_down, 1, 1) * 2.0 * relu).astype(BF16)
    return row_grad, act, pre_grad, dot(pre_grad, w_up, 1, 0).astype(BF16)


def outer(lefts, rights, width, name):
    n = lefts[0].shape[1]
    step = 384
    blocks = n // step

    def kernel(*refs):
        left_refs, right_refs = refs[: len(lefts)], refs[len(lefts) : len(lefts) + len(rights)]
        out, buffer, sems = refs[-3:]
        copies = []
        right = jnp.concatenate([ref[:, :width] for ref in right_refs], axis=0)
        for k in range(blocks):
            rows = pl.ds(k * step, step)
            left = jnp.concatenate([ref[:, k * step : (k + 1) * step] for ref in left_refs], axis=0)
            left = (left * left).astype(BF16) if left.dtype == F32 else left
            buffer[rows] = dot(left, right, 0, 0).astype(BF16)
            copies.append(pltpu.make_async_copy(buffer.at[rows], out.at[0, rows], sems.at[k]))
            copies[-1].start()
        for copy in copies:
            copy.wait()

    return call(kernel, S((1, n, width), BF16), [VMEM] * (len(lefts) + len(rights)), name,
        (pltpu.VMEM((n, width), BF16), pltpu.SemaphoreType.DMA((blocks,))), ANY,
        flops=2 * sum(left.shape[0] for left in lefts) * n * width, moved=2 * n * width)(*lefts, *rights)


def local(latent, out_grad, gates, expert_ids, up_weight, down_weight):
    width = latent.shape[1]
    rows = up_weight.shape[1]
    members = lax.axis_size("member")
    groups = lax.axis_size("group")
    devices = members * groups
    core = (members, members)
    plan = stages(members, devices)
    tokens = latent.shape[0] * devices
    flops = 2 * tokens * rows * width
    small = tokens == 256 and rows % 384 == 0 and len(plan) == 2
    w_up, w_down = up_weight[0], down_weight[0]

    half = tokens // 2
    rows_all = pack(latent, out_grad, gates, expert_ids)
    if not small:
        for masks in plan:
            got = [swap(rows_all, mask, members, devices) for mask in masks]
            rows_all = jnp.concatenate([rows_all] + got, axis=0)
        rows_all = jnp.concatenate([rows_all, swap(rows_all, core, members, devices)], axis=0)
        x = rows_all[:, :width]
        row_grad, act, pre_grad, part = plain(x, rows_all[:, width:], w_up, w_down)
        ours = part[:half].astype(F32)
        got = swap(part[half:], core, members, devices)
    else:
        outs = (S((half, rows), F32), S((half, width), BF16), S((half, rows), BF16))
        rows_all, w_up = tie((rows_all, w_up))
        got = [swap(rows_all, mask, members, devices) for mask in plan[0]]
        w_up, up_turned = load(w_up, "load_up", True)
        got[TIED[0]], w_up, up_turned = tie((got[TIED[0]], w_up, up_turned))
        rows_all = tie(jnp.concatenate([rows_all] + got, axis=0))

        rows_all, w_down = tie((rows_all, w_down))
        got = [swap(rows_all, mask, members, devices) for mask in plan[1]]
        down_turned = load(w_down, "load_down", False)
        got[TIED[1]], down_turned = tie((got[TIED[1]], down_turned))
        rows_all = tie(jnp.concatenate([rows_all] + got, axis=0))

        theirs = swap(rows_all, core, members, devices)
        first = call(hidden, outs, [VMEM] * 3, "hidden", flops=flops)(rows_all, up_turned, down_turned)
        theirs, first = tie((theirs, first))
        second = call(hidden_part, (*outs, S((half, width), BF16)), [VMEM] * 4, "hidden_part", flops=3 * flops // 2)(
            theirs, up_turned, down_turned, w_up)
        got = swap(second[3], core, members, devices)
        ours = call(part_kernel, S((half, width), F32), [VMEM] * 2, "part", flops=flops // 2)(first[2], w_up)
        x = (rows_all, theirs)
        relu, row_grad, pre_grad = ((first[k], second[k]) for k in range(3))

    total = ours + got.astype(F32)
    for k, masks in enumerate(reversed(plan)):
        count = total.shape[0] // (len(masks) + 1)
        cut = [total[j * count : (j + 1) * count] for j in range(len(masks) + 1)]
        got = [swap(block.astype(BF16), mask, members, devices) for block, mask in zip(cut[1:], masks)]
        t = TIED[(2 + k) % 4]
        if small and k == 0:
            up_grad = outer(pre_grad, x, width, "up")
            got[t], up_grad = tie((got[t], up_grad))
        if small and k == 1:
            down_grad = outer(relu, row_grad, width, "down")
            got[t], down_grad = tie((got[t], down_grad))
        total = cut[0] + sum(block.astype(F32) for block in got)
    if not small:
        up_grad = dot(pre_grad, x, 0, 0).astype(BF16)[None]
        down_grad = dot(act, row_grad, 0, 0).astype(BF16)[None]
    return (total, up_grad, down_grad)


def solution(mesh):
    rows = P(AXES, None)
    weights = P("member", "group", None)
    return jax.shard_map(
        local,
        mesh=mesh,
        in_specs=(rows, rows, rows, rows, weights, weights),
        out_specs=(rows, weights, weights),
        check_vma=False,
    )
```
